32 devices in a mesh: dp: 4 (over x, core), seq: 8 (over z, y).
Axes of the slice: x: 2, y: 2, z: 4, core: 2. Of those that a mesh axis runs over, the one named last changes fastest.
Arguments:
- voxels: bfloat16 [4, 1024, 4096], P('dp', 'seq'), may hold values from -6 to 6
- patch_weight: bfloat16 [4096, 1024], replicated, may hold values from -0.09375 to 0.09375
- patch_bias: float32 [1024], replicated, may hold values from -3 to 3
- enc_position: bfloat16 [1024, 1024], P('seq'), may hold values from -5 to 5
- visible: int32 [4, 1024], P('dp', 'seq'), may hold values from 0 to 1, as said below
- enc_project: bfloat16 [1024, 3072], P(('dp', 'seq')), may hold values from -1 to 1
- enc_merge: bfloat16 [1024, 1024], P(('dp', 'seq')), may hold values from -0.1875 to 0.1875
- dec_lift: bfloat16 [1024, 512], P(('dp', 'seq')), may hold values from -0.1875 to 0.1875
- mask_token: float32 [512], replicated, may hold values from -4 to 4
- dec_position: bfloat16 [1024, 512], P('seq'), may hold values from -5 to 5
- dec_project: bfloat16 [512, 1536], P(('dp', 'seq')), may hold values from -1 to 1
- dec_merge: bfloat16 [512, 512], P(('dp', 'seq')), may hold values from -0.25 to 0.25
- dec_predict: bfloat16 [512, 4096], P(('dp', 'seq')), may hold values from -0.25 to 0.25
Outputs:
- decoded: bfloat16 [4, 1024, 512], P('dp', 'seq')
- patch_loss: float32 [4, 1024], P('dp', 'seq')
The draws below stay inside these ranges and needn't reach their ends.
Inputs may be any that keep to these rules, and one draw needn't show every extreme that they name: `visible`: each cube has exactly 256 ones. Each slab of 128 consecutive patches holds between 0 and 64 ones, and in every cube some slab holds exactly 64.
All inputs are finite; a program needn't handle non-finite values.
Results may differ from the reference program's by a relative error of at most 0.008.
Values may be sent and summed in bfloat16 or wider, within the bound.
A program may use at most 128 MiB of HBM per device.

```python
import math
import jax
import jax.numpy as jnp
from jax import lax

D = 1024
ENC_HEADS = 16
DEC = 512
DEC_HEADS = 16
PATCH = 4096
TOK_DEV = 128
TOKENS = 1024
CUBES = 4
VIS = 256


def draw_visible(key, part):
    slabs = TOKENS // TOK_DEV
    half_slabs = slabs // 2
    quarter = TOK_DEV // 4
    key_swing, key_order, key_pick = jax.random.split(jax.random.fold_in(key, 7), 3)
    swing = jax.random.randint(key_swing, (CUBES, half_slabs), 0, quarter + 1)
    swing = swing.at[:, 0].set(quarter)
    paired = jnp.concatenate([quarter + swing, quarter - swing], axis=1)
    orders = jax.vmap(lambda k: jax.random.permutation(k, slabs))(jax.random.split(key_order, CUBES))
    counts = jnp.take_along_axis(paired, orders, axis=1)
    ranks = jax.vmap(lambda k: jax.random.permutation(k, TOK_DEV))(jax.random.split(key_pick, CUBES * slabs))
    ranks = ranks.reshape(CUBES, slabs, TOK_DEV)
    chosen = (ranks < counts[:, :, None]).astype(jnp.int32)
    return chosen.reshape(CUBES, TOKENS)


def position_noise(key, salt, rows, width):
    noise = 0.5 * jax.random.normal(jax.random.fold_in(key, salt + 1), (rows, width), jnp.float32)
    return jnp.clip(noise, -3.0, 3.0)


def project_base(key, salt, width):
    noise = jax.random.normal(jax.random.fold_in(key, salt + 3), (width, 3 * width), jnp.float32)
    return jnp.clip(noise, -6.0, 6.0) / math.sqrt(width)


def draw_enc_position(key, part):
    values = position_noise(key, 101, TOKENS, D)
    return values.astype(jnp.bfloat16)


def draw_dec_position(key, part):
    values = position_noise(key, 201, TOKENS, DEC)
    return values.astype(jnp.bfloat16)


def draw_enc_project(key, part):
    values = project_base(key, 101, D)
    return values.astype(jnp.bfloat16)


def draw_dec_project(key, part):
    values = project_base(key, 201, DEC)
    return values.astype(jnp.bfloat16)


def block_levels(own_key, shape, cuts, low, top_value):
    def one(dim, parts):
        heights = jax.random.uniform(jax.random.fold_in(jax.random.fold_in(own_key, 6), dim), (parts,), jnp.float32, low / len(cuts), top_value / len(cuts))
        return jnp.repeat(jnp.exp(heights), shape[dim] // parts).reshape((-1,) + (1,) * (len(shape) - dim - 1))

    level = one(*cuts[0])
    for cut in cuts[1:]:
        level = level * one(*cut)
    return level


def centred(own_key, shape, scale, most, pieces=(), held_as=jnp.bfloat16):
    array = jax.random.normal(own_key, shape, jnp.float32) * scale
    if len(pieces) > 0:
        array = block_levels(own_key, shape, pieces, -0.22, 0.18) * array
    return jnp.clip(array, min=-most, max=most).astype(held_as)


def setup_inputs(seed: int = 0) -> dict:
    key_list = jax.random.split(jax.random.key(seed), 14)
    voxels = centred(key_list[0], (CUBES, TOKENS, PATCH), 1.0, 6.0, ((0, 4), (1, 8)))
    patch_weight = centred(key_list[1], (PATCH, D), PATCH ** -0.5, 0.09375)
    patch_bias = centred(key_list[2], (D,), 0.5, 3.0, (), jnp.float32)
    enc_position = draw_enc_position(jax.random.fold_in(key_list[13], 71), 0)
    visible = draw_visible(jax.random.fold_in(key_list[13], 71), 0)
    enc_project = draw_enc_project(jax.random.fold_in(key_list[13], 71), 0)
    enc_merge = centred(key_list[6], (D, D), D ** -0.5, 0.1875, ((0, 32),))
    dec_lift = centred(key_list[7], (D, DEC), D ** -0.5, 0.1875, ((0, 32),))
    mask_token = centred(key_list[8], (DEC,), 1.0, 4.0, (), jnp.float32)
    dec_position = draw_dec_position(jax.random.fold_in(key_list[13], 71), 0)
    dec_project = draw_dec_project(jax.random.fold_in(key_list[13], 71), 0)
    dec_merge = centred(key_list[11], (DEC, DEC), DEC ** -0.5, 0.25, ((0, 32),))
    dec_predict = centred(key_list[12], (DEC, PATCH), DEC ** -0.5, 0.25, ((0, 32),))
    return dict(voxels=voxels, patch_weight=patch_weight, patch_bias=patch_bias, enc_position=enc_position, visible=visible, enc_project=enc_project, enc_merge=enc_merge, dec_lift=dec_lift, mask_token=mask_token, dec_position=dec_position, dec_project=dec_project, dec_merge=dec_merge, dec_predict=dec_predict)


def layer_norm(values):
    centre = values - lax.optimization_barrier(jnp.mean(values, axis=-1, keepdims=True))
    spread = lax.optimization_barrier(jnp.mean(centre * centre, axis=-1, keepdims=True))
    return centre * lax.rsqrt(spread + 1e-06)

def attention(packed, heads):
    row_count = packed.shape[0]
    piece_width = packed.shape[1] // 3
    head_size = piece_width // heads
    score_scale = 1.0 / math.sqrt(head_size)
    heads_split = packed.astype(jnp.float32).reshape(row_count, 3, heads, head_size).transpose(1, 2, 0, 3)

    def one_head(triple):
        queries, key_rows, value_rows = triple
        scores = jnp.einsum('qd,kd->qk', queries, key_rows) * score_scale
        top_score = lax.optimization_barrier(jnp.max(scores, axis=-1, keepdims=True))
        exponent = jnp.exp(scores - top_score)
        weights = (exponent / lax.optimization_barrier(jnp.sum(exponent, axis=-1, keepdims=True))).astype(jnp.bfloat16)
        return jnp.einsum('qk,kd->qd', weights.astype(jnp.float32), value_rows).astype(jnp.bfloat16)
    result = lax.map(one_head, (heads_split[0], heads_split[1], heads_split[2]))
    return result.transpose(1, 0, 2).reshape(row_count, piece_width)

def reference(voxels, patch_weight, patch_bias, enc_position, visible, enc_project, enc_merge, dec_lift, mask_token, dec_position, dec_project, dec_merge, dec_predict):

    def one_cube(cube_pair):
        cube_voxels, cube_flags = cube_pair
        embedded = (jnp.dot(cube_voxels, patch_weight, preferred_element_type=jnp.float32) + patch_bias + enc_position.astype(jnp.float32)).astype(jnp.bfloat16)
        kept_order = jnp.argsort(1 - cube_flags, stable=True)[:VIS].astype(jnp.int32)
        kept_rows = embedded[kept_order]
        enc_in = layer_norm(kept_rows.astype(jnp.float32)).astype(jnp.bfloat16)
        packed = jnp.dot(enc_in, enc_project, preferred_element_type=jnp.float32).astype(jnp.bfloat16)
        enc_mix = attention(packed, ENC_HEADS)
        encoded = kept_rows.astype(jnp.float32) + jnp.dot(enc_mix, enc_merge, preferred_element_type=jnp.float32)
        lifted = jnp.dot(layer_norm(encoded).astype(jnp.bfloat16), dec_lift, preferred_element_type=jnp.float32)
        filled = jnp.broadcast_to(mask_token, (TOKENS, DEC)).astype(jnp.float32)
        dec_in = (filled.at[kept_order].set(lifted) + dec_position.astype(jnp.float32)).astype(jnp.bfloat16)
        dec_packed = jnp.dot(layer_norm(dec_in.astype(jnp.float32)).astype(jnp.bfloat16), dec_project, preferred_element_type=jnp.float32).astype(jnp.bfloat16)
        dec_mix = attention(dec_packed, DEC_HEADS)
        decoded = (dec_in.astype(jnp.float32) + jnp.dot(dec_mix, dec_merge, preferred_element_type=jnp.float32)).astype(jnp.bfloat16)
        predicted = jnp.dot(layer_norm(decoded.astype(jnp.float32)).astype(jnp.bfloat16), dec_predict, preferred_element_type=jnp.float32)
        target = layer_norm(cube_voxels.astype(jnp.float32))
        squared = lax.optimization_barrier(jnp.mean((predicted - target) * (predicted - target), axis=-1))
        losses = jnp.where(cube_flags == 1, jnp.zeros_like(squared), squared)
        return (decoded, losses)
    decoded, patch_loss = lax.map(one_cube, (voxels, visible))
    return (decoded, patch_loss)
```

```python
import math

import jax
import jax.numpy as jnp
from jax import lax
from jax.experimental import pallas as pl
from jax.experimental.pallas import tpu as pltpu
from jax.sharding import PartitionSpec as P

ENC_HEADS = 16
DEC_HEADS = 16


def layer_norm(values):
    centre = values - jnp.mean(values, axis=-1, keepdims=True)
    spread = jnp.mean(centre * centre, axis=-1, keepdims=True)
    return centre * lax.rsqrt(spread + 1e-06)


def attend_rows(queries, key_rows, value_rows, key_ok):
    query_rows, local_heads, head_size = queries.shape
    block_rows = math.gcd(query_rows, 512)
    score_scale = 1.0 / math.sqrt(head_size)
    head_outputs = []
    for head_index in range(local_heads):
        query_blocks = queries[:, head_index].reshape(
            query_rows // block_rows, block_rows, head_size
        )
        keys_one = key_rows[:, head_index]
        values_one = value_rows[:, head_index]

        def one_block(query_block):
            scores = (
                jnp.einsum("qd,kd->qk", query_block, keys_one, preferred_element_type=jnp.float32)
                * score_scale
            )
            if key_ok is not None:
                scores = jnp.where(key_ok[None, :], scores, -1e30)
            top_score = jnp.max(scores, axis=-1, keepdims=True)
            exponent = jnp.exp(scores - top_score)
            weights = (exponent / jnp.sum(exponent, axis=-1, keepdims=True)).astype(jnp.bfloat16)
            return jnp.einsum(
                "qk,kd->qd", weights, values_one, preferred_element_type=jnp.float32
            ).astype(jnp.bfloat16)

        head_outputs.append(lax.map(one_block, query_blocks).reshape(query_rows, head_size))
    return jnp.stack(head_outputs, axis=1)


def spread_heads(packed, heads, seq_count):
    row_count = packed.shape[0]
    head_size = packed.shape[1] // (3 * heads)
    query_parts = max(seq_count // heads, 1)
    local_heads = max(heads // seq_count, 1)
    layout = packed.reshape(row_count, 3, heads, head_size)
    if query_parts > 1:
        layout = jnp.repeat(layout, query_parts, axis=2)
    layout = layout.reshape(row_count, 3, seq_count, local_heads, head_size).transpose(
        2, 0, 1, 3, 4
    )
    return layout.reshape(seq_count, row_count, 3 * local_heads * head_size)


def attend_heads(incoming, key_ok, heads, query_part, query_parts):
    sources, row_count, triple_width = incoming.shape
    local_heads = max(heads // sources, 1)
    head_size = triple_width // (3 * local_heads)
    all_rows = sources * row_count
    layout = incoming.reshape(all_rows, 3, local_heads, head_size)
    query_rows = all_rows // query_parts
    queries = lax.dynamic_slice_in_dim(layout[:, 0], query_part * query_rows, query_rows, 0)
    return attend_rows(queries, layout[:, 1], layout[:, 2], key_ok)


def place_rows(mixed_part, all_rows, query_part, sources):
    query_rows = mixed_part.shape[0]
    flat_part = mixed_part.reshape(query_rows, -1)
    buffer = jnp.zeros((all_rows, flat_part.shape[1]), jnp.bfloat16)
    buffer = lax.dynamic_update_slice(buffer, flat_part, (query_part * query_rows, 0))
    return buffer.reshape(sources, all_rows // sources, flat_part.shape[1])


def collect_heads(returned, heads, query_parts):
    sources, row_count, piece_width = returned.shape
    local_heads = max(heads // sources, 1)
    head_size = piece_width // local_heads
    arranged = returned.reshape(sources, row_count, local_heads, head_size).transpose(1, 0, 2, 3)
    arranged = arranged.reshape(row_count, heads, query_parts, head_size)
    summed = jnp.sum(arranged.astype(jnp.float32), axis=2).astype(jnp.bfloat16)
    return summed.reshape(row_count, heads * head_size)


def shards(
    voxels,
    patch_weight,
    patch_bias,
    enc_position,
    visible,
    enc_project,
    enc_merge,
    dec_lift,
    mask_token,
    dec_position,
    dec_project,
    dec_merge,
    dec_predict,
):
    seq_count = lax.axis_size("seq")
    seq_place = lax.axis_index("seq")
    enc_parts = max(seq_count // ENC_HEADS, 1)
    dec_parts = max(seq_count // DEC_HEADS, 1)
    enc_part = seq_place % enc_parts
    dec_part = seq_place % dec_parts
    full_project, full_merge, full_lift = (
        lax.all_gather(enc_project, ("dp", "seq"), axis=0, tiled=True),
        lax.all_gather(enc_merge, ("dp", "seq"), axis=0, tiled=True),
        lax.all_gather(dec_lift, ("dp", "seq"), axis=0, tiled=True),
    )
    tok_local = voxels.shape[1]
    slab_max = tok_local // 2
    slot_ids = jnp.arange(slab_max, dtype=jnp.int32)
    cube_index = 0
    cube_flags = visible[cube_index]
    embedded = (
        jnp.dot(voxels[cube_index], patch_weight, preferred_element_type=jnp.float32)
        + patch_bias
        + enc_position.astype(jnp.float32)
    ).astype(jnp.bfloat16)
    ranking = jnp.cumsum(cube_flags) - 1
    slot_index = jnp.where(cube_flags == 1, ranking, slab_max)
    chooser = (slot_index[None, :] == slot_ids[:, None]).astype(jnp.bfloat16)
    kept_rows = jnp.dot(chooser, embedded, preferred_element_type=jnp.float32).astype(jnp.bfloat16)
    present = slot_ids < jnp.sum(cube_flags)
    packed = jnp.dot(
        layer_norm(kept_rows.astype(jnp.float32)).astype(jnp.bfloat16),
        full_project,
        preferred_element_type=jnp.float32,
    ).astype(jnp.bfloat16)
    key_marks = jnp.broadcast_to(present.astype(jnp.bfloat16)[None, :], (seq_count, slab_max))
    outgoing = spread_heads(packed, ENC_HEADS, seq_count)
    incoming = lax.all_to_all(outgoing, "seq", split_axis=0, concat_axis=0, tiled=True)
    in_marks = lax.all_to_all(key_marks, "seq", split_axis=0, concat_axis=0, tiled=True)
    key_ok = in_marks.reshape(-1) > 0.5
    mixed_part = attend_heads(incoming, key_ok, ENC_HEADS, enc_part, enc_parts)
    returning = place_rows(mixed_part, incoming.shape[0] * incoming.shape[1], enc_part, seq_count)
    returned = lax.all_to_all(returning, "seq", split_axis=0, concat_axis=0, tiled=True)
    mixed_rows = collect_heads(returned, ENC_HEADS, enc_parts)
    encoded = kept_rows.astype(jnp.float32) + jnp.dot(
        mixed_rows, full_merge, preferred_element_type=jnp.float32
    )
    lifted_list = [
        jnp.dot(
            layer_norm(encoded).astype(jnp.bfloat16), full_lift, preferred_element_type=jnp.float32
        )
    ]
    rank_list = [ranking]
    dec_weights = (
        lax.all_gather(dec_project, ("dp", "seq"), axis=0, tiled=True),
        lax.all_gather(dec_merge, ("dp", "seq"), axis=0, tiled=True),
        lax.all_gather(dec_predict, ("dp", "seq"), axis=0, tiled=True),
    )
    cube_index = 0
    cube_flags = visible[cube_index]
    taken_rows = jnp.take(
        lifted_list[cube_index], jnp.clip(rank_list[cube_index], 0, slab_max - 1), axis=0
    )
    dec_in = (
        jnp.where(cube_flags[:, None] == 1, taken_rows, mask_token[None, :])
        + dec_position.astype(jnp.float32)
    ).astype(jnp.bfloat16)
    dec_packed = jnp.dot(
        layer_norm(dec_in.astype(jnp.float32)).astype(jnp.bfloat16),
        dec_weights[0],
        preferred_element_type=jnp.float32,
    ).astype(jnp.bfloat16)
    outgoing = spread_heads(dec_packed, DEC_HEADS, seq_count)
    incoming = lax.all_to_all(outgoing, "seq", split_axis=0, concat_axis=0, tiled=True)
    mixed_part = attend_heads(incoming, None, DEC_HEADS, dec_part, dec_parts)
    returning = place_rows(mixed_part, incoming.shape[0] * incoming.shape[1], dec_part, seq_count)
    returned = lax.all_to_all(returning, "seq", split_axis=0, concat_axis=0, tiled=True)
    mixed_rows = collect_heads(returned, DEC_HEADS, dec_parts)
    decoded = (
        dec_in.astype(jnp.float32)
        + jnp.dot(mixed_rows, dec_weights[1], preferred_element_type=jnp.float32)
    ).astype(jnp.bfloat16)
    predicted = jnp.dot(
        layer_norm(decoded.astype(jnp.float32)).astype(jnp.bfloat16),
        dec_weights[2],
        preferred_element_type=jnp.float32,
    )
    target = layer_norm(voxels[cube_index].astype(jnp.float32))
    squared = jnp.mean((predicted - target) * (predicted - target), axis=-1)
    loss_list = [jnp.where(cube_flags == 1, jnp.zeros_like(squared), squared)]
    decoded_list = [decoded]
    return (jnp.stack(decoded_list), jnp.stack(loss_list))


def norm_rows(values):
    centre = values - jnp.mean(values, axis=-1, keepdims=True)
    spread = jnp.mean(centre * centre, axis=-1, keepdims=True)
    return centre * lax.rsqrt(spread + 1e-06)


def dot32(left, right):
    return jnp.dot(left, right, preferred_element_type=jnp.float32)


def dot_nt(left, right):
    return lax.dot_general(
        left, right, (((1,), (1,)), ((), ())), preferred_element_type=jnp.float32
    )


PIECES = 4
SENDS = 160
MESH = pl.DeviceIdType.MESH


def fused(
    vox_hbm,
    pw_hbm,
    bias_ref,
    epos_hbm,
    vis_ref,
    eproj_hbm,
    emerge_hbm,
    lift_hbm,
    mask_ref,
    dpos_hbm,
    dproj_hbm,
    dmerge_hbm,
    pred_hbm,
    dec_out,
    loss_out,
    vx,
    pw,
    ep,
    dpo,
    flags_buf,
    we,
    wd,
    pos,
    bm,
    bl,
    bd,
    bp,
    e_buf,
    x_buf,
    m1,
    r1,
    m2,
    r2,
    qm,
    qkv,
    lsem,
    ssem,
    rsem,
):
    dp = lax.axis_index("dp")
    sq = lax.axis_index("seq")
    x, c = dp // 2, dp % 2
    z, y = sq // 2, sq % 2
    seq_peers = [(sq + j) % 8 for j in range(1, 8)]
    z_peers = [((z + k) % 4) * 2 + y for k in range(1, 4)]
    z_from = [(z + 4 - k) % 4 for k in range(1, 4)]
    y_dev = (dp, z * 2 + 1 - y)
    x_dev = ((1 - x) * 2 + c, sq)
    c_dev = (x * 2 + 1 - c, sq)

    counter = [0]
    sent = []

    def send(src, dst, device):
        index = counter[0]
        counter[0] += 1
        copy = pltpu.make_async_remote_copy(
            src_ref=src,
            dst_ref=dst,
            send_sem=ssem.at[index],
            recv_sem=rsem.at[index],
            device_id=device,
            device_id_type=MESH,
        )
        copy.start()
        sent.append(copy)
        return copy

    local_count = [0]

    def local(src, dst):
        index = local_count[0]
        local_count[0] += 1
        copy = pltpu.make_async_copy(src, dst, lsem.at[index])
        copy.start()
        return copy

    def landed(copies):
        for copy in copies:
            copy.wait_recv()

    vox_copy = local(vox_hbm, vx)
    rows_piece = 4096 // PIECES
    pw_copies = [
        local(pw_hbm.at[pl.ds(i * rows_piece, rows_piece)], pw.at[pl.ds(i * rows_piece, rows_piece)])
        for i in range(PIECES)
    ]
    ep_copy = local(epos_hbm, ep)
    dpo_copy = local(dpos_hbm, dpo)
    own = []
    for third in range(3):
        own.append(
            local(
                eproj_hbm.at[:, pl.ds(pl.multiple_of(third * 1024 + sq * 128, 128), 128)],
                we.at[third, x, c, sq],
            )
        )
        own.append(
            local(
                dproj_hbm.at[:, pl.ds(pl.multiple_of(third * 512 + z * 128, 128), 128)],
                wd.at[third, x, c, sq],
            )
        )
    own.append(local(dpos_hbm.at[pl.ds(pl.multiple_of(dp * 32, 32), 32)], pos.at[x, c, sq]))
    for part, buf in ((emerge_hbm, bm), (lift_hbm, bl), (dmerge_hbm, bd), (pred_hbm, bp)):
        own.append(local(part, buf.at[x, c, z, y]))

    flag_row = vis_ref[...].astype(jnp.float32)
    flags_buf[sq] = jnp.broadcast_to(flag_row, (8, 128))

    barrier = pltpu.get_barrier_semaphore()
    for peer in seq_peers:
        pl.semaphore_signal(barrier, inc=1, device_id=(dp, peer), device_id_type=MESH)
    pl.semaphore_signal(barrier, inc=1, device_id=x_dev, device_id_type=MESH)
    pl.semaphore_signal(barrier, inc=1, device_id=c_dev, device_id_type=MESH)
    pl.semaphore_wait(barrier, 9)

    we_in, wd_in, pos_in, flags_in = [], [], [], []
    for peer in seq_peers:
        for third in range(3):
            we_in.append(
                send(
                    eproj_hbm.at[:, pl.ds(pl.multiple_of(third * 1024 + peer * 128, 128), 128)],
                    we.at[third, x, c, sq],
                    (dp, peer),
                )
            )
    for peer in seq_peers:
        flags_in.append(send(flags_buf.at[sq], flags_buf.at[sq], (dp, peer)))

    def z_stage(part, buf):
        return [send(part, buf.at[x, c, z, y], (dp, peer)) for peer in z_peers]

    bm_in = z_stage(emerge_hbm, bm)
    bl_in = z_stage(lift_hbm, bl)
    for peer in seq_peers:
        for third in range(3):
            wd_in.append(
                send(
                    dproj_hbm.at[
                        :, pl.ds(pl.multiple_of(third * 512 + (peer // 2) * 128, 128), 128)
                    ],
                    wd.at[third, x, c, sq],
                    (dp, peer),
                )
            )
    for peer in seq_peers:
        pos_in.append(
            send(
                dpos_hbm.at[pl.ds(pl.multiple_of(dp * 32, 32), 32)], pos.at[x, c, sq], (dp, peer)
            )
        )

    tok_col = lax.broadcasted_iota(jnp.int32, (128, 128), 0)
    tok_row = lax.broadcasted_iota(jnp.int32, (128, 128), 1)
    upto = (tok_col <= tok_row).astype(jnp.bfloat16)
    slot_col = lax.broadcasted_iota(jnp.int32, (64, 128), 0).astype(jnp.float32)

    def chooser_of(row):
        rank = dot32(jnp.broadcast_to(row, (8, 128)).astype(jnp.bfloat16), upto)[0:1] - 1.0
        return jnp.where(
            (jnp.broadcast_to(rank, (64, 128)) == slot_col)
            & (jnp.broadcast_to(row, (64, 128)) > 0.5),
            1.0,
            0.0,
        )

    chooser = chooser_of(flag_row).astype(jnp.bfloat16)
    vox_copy.wait()
    total = jnp.zeros((128, 1024), jnp.float32)
    for i in range(PIECES):
        pw_copies[i].wait()
        total = total + dot32(
            vx[:, i * rows_piece : (i + 1) * rows_piece],
            pw[i * rows_piece : (i + 1) * rows_piece, :],
        )
    ep_copy.wait()
    embedded = (total + bias_ref[...] + ep[...].astype(jnp.float32)).astype(jnp.bfloat16)
    kept = dot32(chooser, embedded)
    e_buf[z, y] = norm_rows(kept).astype(jnp.bfloat16)

    e_z = [send(e_buf.at[z, y], e_buf.at[z, y], (dp, peer)) for peer in z_peers]
    e_y = [send(e_buf.at[z, y], e_buf.at[z, y], y_dev)]

    for copy in own:
        copy.wait()
    landed(we_in)
    we_x = send(we.at[:, x, c], we.at[:, x, c], x_dev)

    vox32 = vx[...].astype(jnp.float32)
    vox_mean = jnp.mean(vox32, axis=-1, keepdims=True)
    vox_centre = vox32 - vox_mean
    vox_scale = lax.rsqrt(jnp.mean(vox_centre * vox_centre, axis=-1, keepdims=True) + 1e-06)

    for k in range(3):
        e_z[k].wait_recv()
        e_y.append(send(e_buf.at[z_from[k], y], e_buf.at[z_from[k], y], y_dev))
    we_x.wait_recv()
    we_c = send(we.at[:, :, c], we.at[:, :, c], c_dev)
    landed(bm_in)
    bm_y = send(bm.at[x, c, :, y], bm.at[x, c, :, y], y_dev)
    landed(bl_in)
    bl_y = send(bl.at[x, c, :, y], bl.at[x, c, :, y], y_dev)
    landed(wd_in)
    wd_x = send(wd.at[:, x, c], wd.at[:, x, c], x_dev)
    landed(pos_in)
    pos_x = send(pos.at[x, c], pos.at[x, c], x_dev)
    landed(flags_in)
    flags_all = jnp.max(flags_buf[...], axis=1)
    counts = jnp.sum(flags_all, axis=1, keepdims=True)
    lane512 = lax.broadcasted_iota(jnp.int32, (8, 512), 1)
    slab512 = lax.broadcasted_iota(jnp.int32, (8, 512), 0)
    count_row = jnp.sum(
        jnp.where(lane512 // 64 == slab512, jnp.broadcast_to(counts, (8, 512)), 0.0),
        axis=0,
        keepdims=True,
    )
    key_ok = (lane512[0:1] % 64).astype(jnp.float32) < count_row
    landed(e_y)
    bm_y.wait_recv()
    bm_x = send(bm.at[x, c], bm.at[x, c], x_dev)
    bl_y.wait_recv()
    bl_x = send(bl.at[x, c], bl.at[x, c], x_dev)
    bd_in = z_stage(dmerge_hbm, bd)
    bp_in = z_stage(pred_hbm, bp)
    wd_x.wait_recv()
    wd_c = send(wd.at[:, :, c], wd.at[:, :, c], c_dev)
    pos_x.wait_recv()
    pos_c = send(pos.at[:, c], pos.at[:, c], c_dev)
    we_c.wait_recv()

    rows_in = e_buf[...].reshape(512, 1024)
    q_all, k_all, v_all = (
        dot32(rows_in, we[third].reshape(1024, 128)).astype(jnp.bfloat16) for third in range(3)
    )
    lane128 = lax.broadcasted_iota(jnp.int32, (512, 128), 1)
    results = []
    for head in range(2):
        mine = lane128 // 64 == head
        q_one = jnp.where(mine, q_all, jnp.zeros_like(q_all))
        v_one = jnp.where(mine, v_all, jnp.ones_like(v_all))
        scores = dot_nt(q_one, k_all) * (1.0 / 8.0)
        scores = jnp.where(jnp.broadcast_to(key_ok, (512, 512)), scores, -1e30)
        top = jnp.max(scores, axis=-1, keepdims=True)
        weights = jnp.exp(scores - top).astype(jnp.bfloat16)
        summed = dot32(weights, v_one)
        spot = 64 * (1 - head)
        results.append(summed / summed[:, spot : spot + 1])
    m1[...] = (
        jnp.where(lane128 < 64, results[0], results[1]).astype(jnp.bfloat16).reshape(8, 64, 128)
    )
    r1[sq] = m1[sq]
    r1_in = [send(m1.at[peer], r1.at[sq], (dp, peer)) for peer in seq_peers]

    bm_x.wait_recv()
    bm_c = send(bm.at[:, c], bm.at[:, c], c_dev)
    bl_x.wait_recv()
    bl_c = send(bl.at[:, c], bl.at[:, c], c_dev)
    wd_c.wait_recv()
    pos_c.wait_recv()
    wd_all = jnp.concatenate([wd[third].reshape(512, 128) for third in range(3)], axis=1)
    mask_row = mask_ref[...]

    def masked_slab(slab, carry):
        slab_pos = pos[:, :, slab].reshape(128, 512).astype(jnp.float32)
        slab_in = (mask_row + slab_pos).astype(jnp.bfloat16).astype(jnp.float32)
        qm[slab] = dot32(norm_rows(slab_in).astype(jnp.bfloat16), wd_all).astype(jnp.bfloat16)
        return carry

    lax.fori_loop(0, 8, masked_slab, 0)
    landed(bp_in)
    bp_x = send(bp.at[x, c, :, y], bp.at[x, c, :, y], x_dev)
    landed(bd_in)
    bd_y = send(bd.at[x, c, :, y], bd.at[x, c, :, y], y_dev)
    dpo_copy.wait()
    own_pos = dpo[...]
    slot_pos = dot32(chooser, own_pos)
    landed(r1_in)
    bm_c.wait_recv()
    bl_c.wait_recv()

    mixed = jnp.concatenate([r1[s] for s in range(8)], axis=1)
    encoded = kept + dot32(mixed, bm[...].reshape(1024, 1024))
    lifted = dot32(norm_rows(encoded).astype(jnp.bfloat16), bl[...].reshape(1024, 512))
    slot_in = (lifted + slot_pos).astype(jnp.bfloat16)
    x_buf[z, y] = norm_rows(slot_in.astype(jnp.float32)).astype(jnp.bfloat16)
    x_z = [send(x_buf.at[z, y], x_buf.at[z, y], (dp, peer)) for peer in z_peers]
    x_y = [send(x_buf.at[z, y], x_buf.at[z, y], y_dev)]

    def spread(row):
        return jnp.transpose(chooser_of(row))

    own_spread = spread(flag_row)
    own_flag = jnp.sum(own_spread, axis=1, keepdims=True)
    filled = dot32(own_spread.astype(jnp.bfloat16), slot_in)
    dec_in = jnp.where(
        own_flag > 0.5,
        filled,
        (mask_row + own_pos.astype(jnp.float32)).astype(jnp.bfloat16).astype(jnp.float32),
    )
    bd_y.wait_recv()
    bd_x = send(bd.at[x, c], bd.at[x, c], x_dev)
    for k in range(3):
        x_z[k].wait_recv()
        x_y.append(send(x_buf.at[z_from[k], y], x_buf.at[z_from[k], y], y_dev))
    bp_x.wait_recv()
    landed(x_y)
    bp_y = send(bp.at[:, c, :, y], bp.at[:, c, :, y], y_dev)

    slot_qkv = dot32(x_buf[...].reshape(512, 512), wd_all).astype(jnp.bfloat16)
    for slab in range(8):
        slab_spread = spread(flags_all[slab : slab + 1])
        slab_flag = jnp.sum(slab_spread, axis=1, keepdims=True)
        placed = dot32(slab_spread.astype(jnp.bfloat16), slot_qkv[slab * 64 : slab * 64 + 64])
        qkv[slab * 128 : slab * 128 + 128, :] = jnp.where(
            slab_flag > 0.5, placed, qm[slab].astype(jnp.float32)
        ).astype(jnp.bfloat16)
    bd_x.wait_recv()
    bd_c = send(bd.at[:, c], bd.at[:, c], c_dev)

    lane_q = lax.broadcasted_iota(jnp.int32, (256, 128), 1) // 32
    lane_v = lax.broadcasted_iota(jnp.int32, (1024, 128), 1) // 32
    key_rows = qkv[:, 128:256]
    value_rows = qkv[:, 256:384]
    scale = 1.0 / math.sqrt(32)

    def dec_block(block, carry):
        rows = pl.ds(pl.multiple_of(block * 256, 256), 256)
        q_rows = qkv[rows, 0:128]
        mix = jnp.zeros((256, 128), jnp.float32)
        for head in range(2):
            index = y * 2 + head
            q_one = jnp.where(lane_q == index, q_rows, jnp.zeros_like(q_rows))
            v_one = jnp.where(lane_v == index, value_rows, jnp.ones_like(value_rows))
            scores = dot_nt(q_one, key_rows) * scale
            top = jnp.max(scores, axis=-1, keepdims=True)
            weights = jnp.exp(scores - top).astype(jnp.bfloat16)
            summed = dot32(weights, v_one)
            sums = jnp.where(y == 0, summed[:, 64:65], summed[:, 0:1])
            mix = jnp.where(lane_q == index, summed / sums, mix)
        m2[pl.ds(block * 2, 2)] = mix.astype(jnp.bfloat16).reshape(2, 128, 128)
        return carry

    lax.fori_loop(0, 4, dec_block, 0)
    r2[sq] = m2[sq]
    r2_in = [send(m2.at[peer], r2.at[sq], (dp, peer)) for peer in seq_peers]
    bp_y.wait_recv()
    bp_c = send(bp.at[:, c], bp.at[:, c], c_dev)
    bd_c.wait_recv()
    landed(r2_in)
    dec_mixed = jnp.concatenate([r2[2 * j] + r2[2 * j + 1] for j in range(4)], axis=1)
    decoded = (dec_in + dot32(dec_mixed, bd[...].reshape(512, 512))).astype(jnp.bfloat16)
    dec_out[...] = decoded
    final = norm_rows(decoded.astype(jnp.float32)).astype(jnp.bfloat16)
    bp_c.wait_recv()
    loss = jnp.zeros((128, 1), jnp.float32)
    for piece in range(4):
        cols = slice(piece * 1024, piece * 1024 + 1024)
        predicted = dot32(final, bp[:, :, :, :, :, cols].reshape(512, 1024))
        gap = predicted - (vx[:, cols].astype(jnp.float32) - vox_mean) * vox_scale
        loss = loss + jnp.sum(gap * gap, axis=-1, keepdims=True)
    loss_row = jnp.sum(
        jnp.where(tok_col == tok_row, jnp.broadcast_to(loss * (1.0 / 4096), (128, 128)), 0.0),
        axis=0,
        keepdims=True,
    )
    loss_out[...] = jnp.where(flag_row > 0.5, 0.0, loss_row)
    for copy in sent:
        copy.wait_send()


def fused_shards(
    voxels,
    patch_weight,
    patch_bias,
    enc_position,
    visible,
    enc_project,
    enc_merge,
    dec_lift,
    mask_token,
    dec_position,
    dec_project,
    dec_merge,
    dec_predict,
):
    bf, f32 = jnp.bfloat16, jnp.float32
    hbm = pl.BlockSpec(memory_space=pl.ANY)
    vmem = pl.BlockSpec(memory_space=pltpu.VMEM)
    decoded, loss = pl.pallas_call(
        fused,
        out_shape=(jax.ShapeDtypeStruct((128, 512), bf), jax.ShapeDtypeStruct((1, 128), f32)),
        in_specs=[hbm, hbm, vmem, hbm, vmem, hbm, hbm, hbm, vmem, hbm, hbm, hbm, hbm],
        out_specs=(vmem, vmem),
        scratch_shapes=[
            pltpu.VMEM((128, 4096), bf),
            pltpu.VMEM((4096, 1024), bf),
            pltpu.VMEM((128, 1024), bf),
            pltpu.VMEM((128, 512), bf),
            pltpu.VMEM((8, 8, 128), f32),
            pltpu.VMEM((3, 2, 2, 8, 32, 128), bf),
            pltpu.VMEM((3, 2, 2, 8, 16, 128), bf),
            pltpu.VMEM((2, 2, 8, 32, 512), bf),
            pltpu.VMEM((2, 2, 4, 2, 32, 1024), bf),
            pltpu.VMEM((2, 2, 4, 2, 32, 512), bf),
            pltpu.VMEM((2, 2, 4, 2, 16, 512), bf),
            pltpu.VMEM((2, 2, 4, 2, 16, 4096), bf),
            pltpu.VMEM((4, 2, 64, 1024), bf),
            pltpu.VMEM((4, 2, 64, 512), bf),
            pltpu.VMEM((8, 64, 128), bf),
            pltpu.VMEM((8, 64, 128), bf),
            pltpu.VMEM((8, 128, 128), bf),
            pltpu.VMEM((8, 128, 128), bf),
            pltpu.VMEM((8, 128, 384), bf),
            pltpu.VMEM((1024, 384), bf),
            pltpu.SemaphoreType.DMA((32,)),
            pltpu.SemaphoreType.DMA((SENDS,)),
            pltpu.SemaphoreType.DMA((SENDS,)),
        ],
        compiler_params=pltpu.CompilerParams(
            collective_id=0, has_side_effects=True, vmem_limit_bytes=56 * 2**20
        ),
    )(
        voxels.reshape(128, 4096),
        patch_weight,
        patch_bias.reshape(1, 1024),
        enc_position,
        visible,
        enc_project,
        enc_merge,
        dec_lift,
        mask_token.reshape(1, 512),
        dec_position,
        dec_project,
        dec_merge,
        dec_predict,
    )
    return decoded.reshape(1, 128, 512), loss


def solution(mesh):
    small = mesh.shape["dp"] == 4 and mesh.shape["seq"] == 8
    return jax.shard_map(
        fused_shards if small else shards,
        mesh=mesh,
        in_specs=(
            P("dp", "seq", None),
            P(),
            P(),
            P("seq", None),
            P("dp", "seq"),
            P(("dp", "seq"), None),
            P(("dp", "seq"), None),
            P(("dp", "seq"), None),
            P(),
            P("seq", None),
            P(("dp", "seq"), None),
            P(("dp", "seq"), None),
            P(("dp", "seq"), None),
        ),
        out_specs=(P("dp", "seq", None), P("dp", "seq")),
        check_vma=False,
    )
```

```python
import math

import jax
import jax.numpy as jnp
from jax import lax
from jax.experimental import pallas as pl
from jax.experimental.pallas import tpu as pltpu
from jax.sharding import PartitionSpec as P

ENC_HEADS = 16
DEC_HEADS = 16


def layer_norm(values):
    centre = values - jnp.mean(values, axis=-1, keepdims=True)
    spread = jnp.mean(centre * centre, axis=-1, keepdims=True)
    return centre * lax.rsqrt(spread + 1e-06)


def attend_rows(queries, key_rows, value_rows, key_ok):
    query_rows, local_heads, head_size = queries.shape
    block_rows = math.gcd(query_rows, 512)
    score_scale = 1.0 / math.sqrt(head_size)
    head_outputs = []
    for head_index in range(local_heads):
        query_blocks = queries[:, head_index].reshape(
            query_rows // block_rows, block_rows, head_size
        )
        keys_one = key_rows[:, head_index]
        values_one = value_rows[:, head_index]

        def one_block(query_block):
            scores = (
                jnp.einsum("qd,kd->qk", query_block, keys_one, preferred_element_type=jnp.float32)
                * score_scale
            )
            if key_ok is not None:
                scores = jnp.where(key_ok[None, :], scores, -1e30)
            top_score = jnp.max(scores, axis=-1, keepdims=True)
            exponent = jnp.exp(scores - top_score)
            weights = (exponent / jnp.sum(exponent, axis=-1, keepdims=True)).astype(jnp.bfloat16)
            return jnp.einsum(
                "qk,kd->qd", weights, values_one, preferred_element_type=jnp.float32
            ).astype(jnp.bfloat16)

        head_outputs.append(lax.map(one_block, query_blocks).reshape(query_rows, head_size))
    return jnp.stack(head_outputs, axis=1)


def spread_heads(packed, heads, seq_count):
    row_count = packed.shape[0]
    head_size = packed.shape[1] // (3 * heads)
    query_parts = max(seq_count // heads, 1)
    local_heads = max(heads // seq_count, 1)
    layout = packed.reshape(row_count, 3, heads, head_size)
    if query_parts > 1:
        layout = jnp.repeat(layout, query_parts, axis=2)
    layout = layout.reshape(row_count, 3, seq_count, local_heads, head_size).transpose(
        2, 0, 1, 3, 4
    )
    return layout.reshape(seq_count, row_count, 3 * local_heads * head_size)


def attend_heads(incoming, key_ok, heads, query_part, query_parts):
    sources, row_count, triple_width = incoming.shape
    local_heads = max(heads // sources, 1)
    head_size = triple_width // (3 * local_heads)
    all_rows = sources * row_count
    layout = incoming.reshape(all_rows, 3, local_heads, head_size)
    query_rows = all_rows // query_parts
    queries = lax.dynamic_slice_in_dim(layout[:, 0], query_part * query_rows, query_rows, 0)
    return attend_rows(queries, layout[:, 1], layout[:, 2], key_ok)


def place_rows(mixed_part, all_rows, query_part, sources):
    query_rows = mixed_part.shape[0]
    flat_part = mixed_part.reshape(query_rows, -1)
    buffer = jnp.zeros((all_rows, flat_part.shape[1]), jnp.bfloat16)
    buffer = lax.dynamic_update_slice(buffer, flat_part, (query_part * query_rows, 0))
    return buffer.reshape(sources, all_rows // sources, flat_part.shape[1])


def collect_heads(returned, heads, query_parts):
    sources, row_count, piece_width = returned.shape
    local_heads = max(heads // sources, 1)
    head_size = piece_width // local_heads
    arranged = returned.reshape(sources, row_count, local_heads, head_size).transpose(1, 0, 2, 3)
    arranged = arranged.reshape(row_count, heads, query_parts, head_size)
    summed = jnp.sum(arranged.astype(jnp.float32), axis=2).astype(jnp.bfloat16)
    return summed.reshape(row_count, heads * head_size)


def shards(
    voxels,
    patch_weight,
    patch_bias,
    enc_position,
    visible,
    enc_project,
    enc_merge,
    dec_lift,
    mask_token,
    dec_position,
    dec_project,
    dec_merge,
    dec_predict,
):
    seq_count = lax.axis_size("seq")
    seq_place = lax.axis_index("seq")
    enc_parts = max(seq_count // ENC_HEADS, 1)
    dec_parts = max(seq_count // DEC_HEADS, 1)
    enc_part = seq_place % enc_parts
    dec_part = seq_place % dec_parts
    full_project, full_merge, full_lift = (
        lax.all_gather(enc_project, ("dp", "seq"), axis=0, tiled=True),
        lax.all_gather(enc_merge, ("dp", "seq"), axis=0, tiled=True),
        lax.all_gather(dec_lift, ("dp", "seq"), axis=0, tiled=True),
    )
    tok_local = voxels.shape[1]
    slab_max = tok_local // 2
    slot_ids = jnp.arange(slab_max, dtype=jnp.int32)
    cube_index = 0
    cube_flags = visible[cube_index]
    embedded = (
        jnp.dot(voxels[cube_index], patch_weight, preferred_element_type=jnp.float32)
        + patch_bias
        + enc_position.astype(jnp.float32)
    ).astype(jnp.bfloat16)
    ranking = jnp.cumsum(cube_flags) - 1
    slot_index = jnp.where(cube_flags == 1, ranking, slab_max)
    chooser = (slot_index[None, :] == slot_ids[:, None]).astype(jnp.bfloat16)
    kept_rows = jnp.dot(chooser, embedded, preferred_element_type=jnp.float32).astype(jnp.bfloat16)
    present = slot_ids < jnp.sum(cube_flags)
    packed = jnp.dot(
        layer_norm(kept_rows.astype(jnp.float32)).astype(jnp.bfloat16),
        full_project,
        preferred_element_type=jnp.float32,
    ).astype(jnp.bfloat16)
    key_marks = jnp.broadcast_to(present.astype(jnp.bfloat16)[None, :], (seq_count, slab_max))
    outgoing = spread_heads(packed, ENC_HEADS, seq_count)
    incoming = lax.all_to_all(outgoing, "seq", split_axis=0, concat_axis=0, tiled=True)
    in_marks = lax.all_to_all(key_marks, "seq", split_axis=0, concat_axis=0, tiled=True)
    key_ok = in_marks.reshape(-1) > 0.5
    mixed_part = attend_heads(incoming, key_ok, ENC_HEADS, enc_part, enc_parts)
    returning = place_rows(mixed_part, incoming.shape[0] * incoming.shape[1], enc_part, seq_count)
    returned = lax.all_to_all(returning, "seq", split_axis=0, concat_axis=0, tiled=True)
    mixed_rows = collect_heads(returned, ENC_HEADS, enc_parts)
    encoded = kept_rows.astype(jnp.float32) + jnp.dot(
        mixed_rows, full_merge, preferred_element_type=jnp.float32
    )
    lifted_list = [
        jnp.dot(
            layer_norm(encoded).astype(jnp.bfloat16), full_lift, preferred_element_type=jnp.float32
        )
    ]
    rank_list = [ranking]
    dec_weights = (
        lax.all_gather(dec_project, ("dp", "seq"), axis=0, tiled=True),
        lax.all_gather(dec_merge, ("dp", "seq"), axis=0, tiled=True),
        lax.all_gather(dec_predict, ("dp", "seq"), axis=0, tiled=True),
    )
    cube_index = 0
    cube_flags = visible[cube_index]
    taken_rows = jnp.take(
        lifted_list[cube_index], jnp.clip(rank_list[cube_index], 0, slab_max - 1), axis=0
    )
    dec_in = (
        jnp.where(cube_flags[:, None] == 1, taken_rows, mask_token[None, :])
        + dec_position.astype(jnp.float32)
    ).astype(jnp.bfloat16)
    dec_packed = jnp.dot(
        layer_norm(dec_in.astype(jnp.float32)).astype(jnp.bfloat16),
        dec_weights[0],
        preferred_element_type=jnp.float32,
    ).astype(jnp.bfloat16)
    outgoing = spread_heads(dec_packed, DEC_HEADS, seq_count)
    incoming = lax.all_to_all(outgoing, "seq", split_axis=0, concat_axis=0, tiled=True)
    mixed_part = attend_heads(incoming, None, DEC_HEADS, dec_part, dec_parts)
    returning = place_rows(mixed_part, incoming.shape[0] * incoming.shape[1], dec_part, seq_count)
    returned = lax.all_to_all(returning, "seq", split_axis=0, concat_axis=0, tiled=True)
    mixed_rows = collect_heads(returned, DEC_HEADS, dec_parts)
    decoded = (
        dec_in.astype(jnp.float32)
        + jnp.dot(mixed_rows, dec_weights[1], preferred_element_type=jnp.float32)
    ).astype(jnp.bfloat16)
    predicted = jnp.dot(
        layer_norm(decoded.astype(jnp.float32)).astype(jnp.bfloat16),
        dec_weights[2],
        preferred_element_type=jnp.float32,
    )
    target = layer_norm(voxels[cube_index].astype(jnp.float32))
    squared = jnp.mean((predicted - target) * (predicted - target), axis=-1)
    loss_list = [jnp.where(cube_flags == 1, jnp.zeros_like(squared), squared)]
    decoded_list = [decoded]
    return (jnp.stack(decoded_list), jnp.stack(loss_list))


def norm_rows(values):
    centre = values - jnp.mean(values, axis=-1, keepdims=True)
    spread = jnp.mean(centre * centre, axis=-1, keepdims=True)
    return centre * lax.rsqrt(spread + 1e-06)


def dot32(left, right):
    return jnp.dot(left, right, preferred_element_type=jnp.float32)


def dot_nt(left, right):
    return lax.dot_general(
        left, right, (((1,), (1,)), ((), ())), preferred_element_type=jnp.float32
    )


PIECES = 4
LOG2E = 1.4426950408889634
SENDS = 160
MESH = pl.DeviceIdType.MESH


def fused(
    vox_hbm,
    pw_hbm,
    bias_ref,
    epos_hbm,
    vis_ref,
    eproj_hbm,
    emerge_hbm,
    lift_hbm,
    mask_ref,
    dpos_hbm,
    dproj_hbm,
    dmerge_hbm,
    pred_hbm,
    dec_out,
    loss_out,
    vx,
    pw,
    ep,
    dpo,
    flags_buf,
    we,
    wd,
    pos,
    bm,
    bl,
    bd,
    bpa,
    bpb,
    e_buf,
    x_buf,
    m1,
    r1,
    m2,
    r2,
    qm,
    qkv,
    lsem,
    ssem,
    rsem,
):
    dp = lax.axis_index("dp")
    sq = lax.axis_index("seq")
    x, c = dp // 2, dp % 2
    z, y = sq // 2, sq % 2
    seq_peers = [(sq + j) % 8 for j in range(1, 8)]
    z_peers = [((z + k) % 4) * 2 + y for k in range(1, 4)]
    z_from = [(z + 4 - k) % 4 for k in range(1, 4)]
    y_dev = (dp, z * 2 + 1 - y)
    x_dev = ((1 - x) * 2 + c, sq)
    c_dev = (x * 2 + 1 - c, sq)

    counter = [0]
    sent = []

    def send(src, dst, device):
        index = counter[0]
        counter[0] += 1
        copy = pltpu.make_async_remote_copy(
            src_ref=src,
            dst_ref=dst,
            send_sem=ssem.at[index],
            recv_sem=rsem.at[index],
            device_id=device,
            device_id_type=MESH,
        )
        copy.start()
        sent.append(copy)
        return copy

    local_count = [0]

    def local(src, dst):
        index = local_count[0]
        local_count[0] += 1
        copy = pltpu.make_async_copy(src, dst, lsem.at[index])
        copy.start()
        return copy

    def landed(copies):
        for copy in copies:
            copy.wait_recv()

    vox_copy = local(vox_hbm, vx)
    rows_piece = 4096 // PIECES
    pw_copies = [
        local(pw_hbm.at[pl.ds(i * rows_piece, rows_piece)], pw.at[pl.ds(i * rows_piece, rows_piece)])
        for i in range(PIECES)
    ]
    ep_copy = local(epos_hbm, ep)
    dpo_copy = local(dpos_hbm, dpo)
    own = []
    for third in range(3):
        own.append(
            local(
                eproj_hbm.at[:, pl.ds(pl.multiple_of(third * 1024 + sq * 128, 128), 128)],
                we.at[third, x, c, sq],
            )
        )
        own.append(
            local(
                dproj_hbm.at[:, pl.ds(pl.multiple_of(third * 512 + z * 128, 128), 128)],
                wd.at[third, x, c, sq],
            )
        )
    pos_part = dpos_hbm.at[pl.ds(pl.multiple_of(dp * 32, 32), 32)]
    pred_a, pred_b = pred_hbm.at[:, pl.ds(0, 2048)], pred_hbm.at[:, pl.ds(2048, 2048)]
    for part, buf in (
        (emerge_hbm, bm),
        (lift_hbm, bl),
        (pos_part, pos),
        (dmerge_hbm, bd),
        (pred_a, bpa),
        (pred_b, bpb),
    ):
        own.append(local(part, buf.at[x, c, z, y]))

    flag_row = vis_ref[...].astype(jnp.float32)
    flags_buf[sq] = jnp.broadcast_to(flag_row, (8, 128))

    barrier = pltpu.get_barrier_semaphore()
    for peer in seq_peers:
        pl.semaphore_signal(barrier, inc=1, device_id=(dp, peer), device_id_type=MESH)
    pl.semaphore_signal(barrier, inc=1, device_id=x_dev, device_id_type=MESH)
    pl.semaphore_signal(barrier, inc=1, device_id=c_dev, device_id_type=MESH)
    pl.semaphore_wait(barrier, 9)

    we_in, wd_in, flags_in = [], [], []
    for peer in seq_peers:
        for third in range(3):
            we_in.append(
                send(
                    eproj_hbm.at[:, pl.ds(pl.multiple_of(third * 1024 + peer * 128, 128), 128)],
                    we.at[third, x, c, sq],
                    (dp, peer),
                )
            )
    for peer in seq_peers:
        flags_in.append(send(flags_buf.at[sq], flags_buf.at[sq], (dp, peer)))

    def z_stage(part, buf):
        return [send(part, buf.at[x, c, z, y], (dp, peer)) for peer in z_peers]

    def line(buf, device):
        return send(buf.at[x, c, :, y], buf.at[x, c, :, y], device)

    def sheet_x(buf):
        return send(buf.at[x, c], buf.at[x, c], x_dev)

    def sheet_y(buf):
        return send(buf.at[:, c, :, y], buf.at[:, c, :, y], y_dev)

    def half_c(buf):
        return send(buf.at[:, c], buf.at[:, c], c_dev)

    bm_in = z_stage(emerge_hbm, bm)
    bl_in = z_stage(lift_hbm, bl)
    tok_col = lax.broadcasted_iota(jnp.int32, (128, 128), 0)
    tok_row = lax.broadcasted_iota(jnp.int32, (128, 128), 1)
    upto = (tok_col <= tok_row).astype(jnp.bfloat16)
    slot_col = lax.broadcasted_iota(jnp.int32, (64, 128), 0).astype(jnp.float32)

    def chooser_of(row):
        rank = dot32(jnp.broadcast_to(row, (8, 128)).astype(jnp.bfloat16), upto)[0:1] - 1.0
        return jnp.where(
            (jnp.broadcast_to(rank, (64, 128)) == slot_col)
            & (jnp.broadcast_to(row, (64, 128)) > 0.5),
            1.0,
            0.0,
        )

    chooser = chooser_of(flag_row).astype(jnp.bfloat16)
    vox_copy.wait()
    total = jnp.zeros((128, 1024), jnp.float32)
    for i in range(PIECES):
        pw_copies[i].wait()
        total = total + dot32(
            vx[:, i * rows_piece : (i + 1) * rows_piece],
            pw[i * rows_piece : (i + 1) * rows_piece, :],
        )
    ep_copy.wait()
    embedded = (total + bias_ref[...] + ep[...].astype(jnp.float32)).astype(jnp.bfloat16)
    kept = dot32(chooser, embedded)
    e_buf[z, y] = norm_rows(kept).astype(jnp.bfloat16)

    e_z = [send(e_buf.at[z, y], e_buf.at[z, y], (dp, peer)) for peer in z_peers]
    e_y = [send(e_buf.at[z, y], e_buf.at[z, y], y_dev)]

    for peer in seq_peers:
        for third in range(3):
            wd_in.append(
                send(
                    dproj_hbm.at[
                        :, pl.ds(pl.multiple_of(third * 512 + (peer // 2) * 128, 128), 128)
                    ],
                    wd.at[third, x, c, sq],
                    (dp, peer),
                )
            )
    pos_in = z_stage(pos_part, pos)

    for copy in own:
        copy.wait()
    landed(we_in)
    we_x = send(we.at[:, x, c], we.at[:, x, c], x_dev)
    landed(bl_in)
    bl_x = line(bl, x_dev)
    landed(bm_in)
    bm_y = line(bm, y_dev)

    vox32 = vx[...].astype(jnp.float32)
    vox_mean = jnp.mean(vox32, axis=-1, keepdims=True)
    vox_centre = vox32 - vox_mean
    vox_scale = lax.rsqrt(jnp.mean(vox_centre * vox_centre, axis=-1, keepdims=True) + 1e-06)

    we_x.wait_recv()
    we_c = send(we.at[:, :, c], we.at[:, :, c], c_dev)
    bm_y.wait_recv()
    bm_x = sheet_x(bm)
    for k in range(3):
        e_z[k].wait_recv()
        e_y.append(send(e_buf.at[z_from[k], y], e_buf.at[z_from[k], y], y_dev))
    bl_x.wait_recv()
    bl_y = sheet_y(bl)
    landed(flags_in)
    flags_all = jnp.max(flags_buf[...], axis=1)
    counts = jnp.sum(flags_all, axis=1, keepdims=True)
    lane512 = lax.broadcasted_iota(jnp.int32, (8, 512), 1)
    slab512 = lax.broadcasted_iota(jnp.int32, (8, 512), 0)
    count_row = jnp.sum(
        jnp.where(lane512 // 64 == slab512, jnp.broadcast_to(counts, (8, 512)), 0.0),
        axis=0,
        keepdims=True,
    )
    key_ok = (lane512[0:1] % 64).astype(jnp.float32) < count_row
    landed(e_y)
    bpb_in = z_stage(pred_b, bpb)
    bpa_in = z_stage(pred_a, bpa)
    bd_in = z_stage(dmerge_hbm, bd)
    we_c.wait_recv()

    rows_in = e_buf[...].reshape(512, 1024)
    q_all, k_all, v_all = (
        dot32(rows_in, we[third].reshape(1024, 128)).astype(jnp.bfloat16) for third in range(3)
    )
    lane128 = lax.broadcasted_iota(jnp.int32, (512, 128), 1)
    results = []
    for head in range(2):
        mine = lane128 // 64 == head
        q_one = jnp.where(mine, q_all, jnp.zeros_like(q_all))
        v_one = jnp.where(mine, v_all, jnp.ones_like(v_all))
        scores = dot_nt(q_one, k_all)
        scores = jnp.where(jnp.broadcast_to(key_ok, (512, 512)), scores, -3e38)
        top = jnp.max(scores, axis=-1, keepdims=True)
        weights = jnp.exp2((scores - top) * (LOG2E / 8.0)).astype(jnp.bfloat16)
        summed = dot32(weights, v_one)
        spot = 64 * (1 - head)
        results.append(summed / summed[:, spot : spot + 1])
    m1[...] = (
        jnp.where(lane128 < 64, results[0], results[1]).astype(jnp.bfloat16).reshape(8, 64, 128)
    )
    r1[sq] = m1[sq]
    r1_in = [send(m1.at[peer], r1.at[sq], (dp, peer)) for peer in seq_peers]

    bm_x.wait_recv()
    bm_c = half_c(bm)
    bl_y.wait_recv()
    bl_c = half_c(bl)
    landed(wd_in)
    wd_x = send(wd.at[:, x, c], wd.at[:, x, c], x_dev)
    landed(pos_in)
    pos_y = line(pos, y_dev)
    landed(bpb_in)
    bpb_y = line(bpb, y_dev)
    landed(bpa_in)
    bpa_x = line(bpa, x_dev)
    landed(bd_in)
    bd_y = line(bd, y_dev)
    wd_x.wait_recv()
    wd_c = send(wd.at[:, :, c], wd.at[:, :, c], c_dev)
    pos_y.wait_recv()
    pos_x = sheet_x(pos)
    mask_row = mask_ref[...]
    dpo_copy.wait()
    own_pos = dpo[...]
    slot_pos = dot32(chooser, own_pos)
    landed(r1_in)
    bm_c.wait_recv()
    bl_c.wait_recv()

    mixed = jnp.concatenate([r1[s] for s in range(8)], axis=1)
    encoded = kept + dot32(mixed, bm[...].reshape(1024, 1024))
    lifted = dot32(norm_rows(encoded).astype(jnp.bfloat16), bl[...].reshape(1024, 512))
    slot_in = (lifted + slot_pos).astype(jnp.bfloat16)
    x_buf[z, y] = norm_rows(slot_in.astype(jnp.float32)).astype(jnp.bfloat16)
    x_z = [send(x_buf.at[z, y], x_buf.at[z, y], (dp, peer)) for peer in z_peers]
    x_y = [send(x_buf.at[z, y], x_buf.at[z, y], y_dev)]

    def spread(row):
        return jnp.transpose(chooser_of(row))

    pos_x.wait_recv()
    pos_c = half_c(pos)
    bpb_y.wait_recv()
    bpb_x = sheet_x(bpb)
    bd_y.wait_recv()
    bd_x = sheet_x(bd)
    own_spread = spread(flag_row)
    own_flag = jnp.sum(own_spread, axis=1, keepdims=True)
    filled = dot32(own_spread.astype(jnp.bfloat16), slot_in)
    dec_in = jnp.where(
        own_flag > 0.5,
        filled,
        (mask_row + own_pos.astype(jnp.float32)).astype(jnp.bfloat16).astype(jnp.float32),
    )
    wd_c.wait_recv()
    wd_all = jnp.concatenate([wd[third].reshape(512, 128) for third in range(3)], axis=1)
    for k in range(3):
        x_z[k].wait_recv()
        x_y.append(send(x_buf.at[z_from[k], y], x_buf.at[z_from[k], y], y_dev))
    bpa_x.wait_recv()
    bpa_y = sheet_y(bpa)
    pos_c.wait_recv()

    def masked_slab(slab, carry):
        slab_pos = pos[:, :, slab // 2, slab % 2].reshape(128, 512).astype(jnp.float32)
        slab_in = (mask_row + slab_pos).astype(jnp.bfloat16).astype(jnp.float32)
        qm[slab] = dot32(norm_rows(slab_in).astype(jnp.bfloat16), wd_all).astype(jnp.bfloat16)
        return carry

    lax.fori_loop(0, 8, masked_slab, 0)
    landed(x_y)

    slot_qkv = dot32(x_buf[...].reshape(512, 512), wd_all).astype(jnp.bfloat16)
    for slab in range(8):
        slab_spread = spread(flags_all[slab : slab + 1])
        slab_flag = jnp.sum(slab_spread, axis=1, keepdims=True)
        placed = dot32(slab_spread.astype(jnp.bfloat16), slot_qkv[slab * 64 : slab * 64 + 64])
        qkv[slab * 128 : slab * 128 + 128, :] = jnp.where(
            slab_flag > 0.5, placed, qm[slab].astype(jnp.float32)
        ).astype(jnp.bfloat16)
    bd_x.wait_recv()
    bd_c = half_c(bd)
    bpb_x.wait_recv()
    bpb_c = half_c(bpb)

    lane_q = lax.broadcasted_iota(jnp.int32, (256, 128), 1) // 32
    lane_v = lax.broadcasted_iota(jnp.int32, (1024, 128), 1) // 32
    key_rows = qkv[:, 128:256]
    value_rows = qkv[:, 256:384]
    scale = LOG2E / math.sqrt(32)

    def dec_block(block, carry):
        rows = pl.ds(pl.multiple_of(block * 256, 256), 256)
        q_rows = qkv[rows, 0:128]
        mix = jnp.zeros((256, 128), jnp.float32)
        for head in range(2):
            index = y * 2 + head
            q_one = jnp.where(lane_q == index, q_rows, jnp.zeros_like(q_rows))
            v_one = jnp.where(lane_v == index, value_rows, jnp.ones_like(value_rows))
            scores = dot_nt(q_one, key_rows)
            top = jnp.max(scores, axis=-1, keepdims=True)
            weights = jnp.exp2((scores - top) * scale).astype(jnp.bfloat16)
            summed = dot32(weights, v_one)
            sums = jnp.where(y == 0, summed[:, 64:65], summed[:, 0:1])
            mix = jnp.where(lane_q == index, summed / sums, mix)
        m2[pl.ds(block * 2, 2)] = mix.astype(jnp.bfloat16).reshape(2, 128, 128)
        return carry

    lax.fori_loop(0, 4, dec_block, 0)
    r2[sq] = m2[sq]
    r2_in = [send(m2.at[peer], r2.at[sq], (dp, peer)) for peer in seq_peers]
    bpa_y.wait_recv()
    bpa_c = half_c(bpa)
    bd_c.wait_recv()
    landed(r2_in)
    dec_mixed = jnp.concatenate([r2[2 * j] + r2[2 * j + 1] for j in range(4)], axis=1)
    decoded = (dec_in + dot32(dec_mixed, bd[...].reshape(512, 512))).astype(jnp.bfloat16)
    dec_out[...] = decoded
    final = norm_rows(decoded.astype(jnp.float32)).astype(jnp.bfloat16)
    loss = jnp.zeros((128, 1), jnp.float32)
    for half, copy, start in ((bpb, bpb_c, 2048), (bpa, bpa_c, 0)):
        copy.wait_recv()
        for piece in range(2):
            predicted = dot32(
                final, half[:, :, :, :, :, piece * 1024 : piece * 1024 + 1024].reshape(512, 1024)
            )
            base = start + piece * 1024
            gap = (
                predicted - (vx[:, base : base + 1024].astype(jnp.float32) - vox_mean) * vox_scale
            )
            loss = loss + jnp.sum(gap * gap, axis=-1, keepdims=True)
    loss_row = jnp.sum(
        jnp.where(tok_col == tok_row, jnp.broadcast_to(loss * (1.0 / 4096), (128, 128)), 0.0),
        axis=0,
        keepdims=True,
    )
    loss_out[...] = jnp.where(flag_row > 0.5, 0.0, loss_row)
    for copy in sent:
        copy.wait_send()


def fused_shards(
    voxels,
    patch_weight,
    patch_bias,
    enc_position,
    visible,
    enc_project,
    enc_merge,
    dec_lift,
    mask_token,
    dec_position,
    dec_project,
    dec_merge,
    dec_predict,
):
    bf, f32 = jnp.bfloat16, jnp.float32
    hbm = pl.BlockSpec(memory_space=pl.ANY)
    vmem = pl.BlockSpec(memory_space=pltpu.VMEM)
    decoded, loss = pl.pallas_call(
        fused,
        out_shape=(jax.ShapeDtypeStruct((128, 512), bf), jax.ShapeDtypeStruct((1, 128), f32)),
        in_specs=[hbm, hbm, vmem, hbm, vmem, hbm, hbm, hbm, vmem, hbm, hbm, hbm, hbm],
        out_specs=(vmem, vmem),
        scratch_shapes=[
            pltpu.VMEM((128, 4096), bf),
            pltpu.VMEM((4096, 1024), bf),
            pltpu.VMEM((128, 1024), bf),
            pltpu.VMEM((128, 512), bf),
            pltpu.VMEM((8, 8, 128), f32),
            pltpu.VMEM((3, 2, 2, 8, 32, 128), bf),
            pltpu.VMEM((3, 2, 2, 8, 16, 128), bf),
            pltpu.VMEM((2, 2, 4, 2, 32, 512), bf),
            pltpu.VMEM((2, 2, 4, 2, 32, 1024), bf),
            pltpu.VMEM((2, 2, 4, 2, 32, 512), bf),
            pltpu.VMEM((2, 2, 4, 2, 16, 512), bf),
            pltpu.VMEM((2, 2, 4, 2, 16, 2048), bf),
            pltpu.VMEM((2, 2, 4, 2, 16, 2048), bf),
            pltpu.VMEM((4, 2, 64, 1024), bf),
            pltpu.VMEM((4, 2, 64, 512), bf),
            pltpu.VMEM((8, 64, 128), bf),
            pltpu.VMEM((8, 64, 128), bf),
            pltpu.VMEM((8, 128, 128), bf),
            pltpu.VMEM((8, 128, 128), bf),
            pltpu.VMEM((8, 128, 384), bf),
            pltpu.VMEM((1024, 384), bf),
            pltpu.SemaphoreType.DMA((32,)),
            pltpu.SemaphoreType.DMA((SENDS,)),
            pltpu.SemaphoreType.DMA((SENDS,)),
        ],
        compiler_params=pltpu.CompilerParams(
            collective_id=0, has_side_effects=True, vmem_limit_bytes=56 * 2**20
        ),
    )(
        voxels.reshape(128, 4096),
        patch_weight,
        patch_bias.reshape(1, 1024),
        enc_position,
        visible,
        enc_project,
        enc_merge,
        dec_lift,
        mask_token.reshape(1, 512),
        dec_position,
        dec_project,
        dec_merge,
        dec_predict,
    )
    return decoded.reshape(1, 128, 512), loss


def solution(mesh):
    small = mesh.shape["dp"] == 4 and mesh.shape["seq"] == 8
    return jax.shard_map(
        fused_shards if small else shards,
        mesh=mesh,
        in_specs=(
            P("dp", "seq", None),
            P(),
            P(),
            P("seq", None),
            P("dp", "seq"),
            P(("dp", "seq"), None),
            P(("dp", "seq"), None),
            P(("dp", "seq"), None),
            P(),
            P("seq", None),
            P(("dp", "seq"), None),
            P(("dp", "seq"), None),
            P(("dp", "seq"), None),
        ),
        out_specs=(P("dp", "seq", None), P("dp", "seq")),
        check_vma=False,
    )
```
